32 devices in a mesh: cells: 8 (over z, x), ens: 4 (over y, core).
Axes of the slice: x: 2, y: 2, z: 4, core: 2. Of those that a mesh axis runs over, the one named last changes fastest.
Arguments:
- state_mean: float32 [16384], P('cells'), may hold values from -6 to 6
- state_pert: float32 [256, 16384], P('ens', 'cells'), may hold values from -6 to 6
- obs_value: float32 [4, 512], P(None, 'cells'), may hold values from -10 to 10
- obs_error: float32 [4, 512], P(None, 'cells'), may hold values from 0.1 to 2
- obs_cell: int32 [4, 512], replicated, may hold values from 0 to 16383, as said below
- block_obs: int32 [4, 32, 96], P(None, 'cells'), may hold values from 0 to 511, as said below
- block_count: int32 [4, 32], P(None, 'cells'), may hold values from 0 to 96, as said below
- batch_order: int32 [4], replicated, may hold values from 0 to 3, each once
Outputs:
- mean_out: float32 [16384], P('cells')
- pert_out: float32 [256, 16384], P('ens', 'cells')
The draws below stay inside these ranges and needn't reach their ends.
Inputs may be any that keep to these rules, and one draw needn't show every extreme that they name: `obs_cell`: each batch's entries are ordered by owner, 64 to an owner, each owner's in nondecreasing blocks; at most 32 observations of a batch lie in one block and at most 16 of one owner's in the cells of one index of cells, both reached in every batch. `block_obs`: entries l < block_count[b, B] are the observations of batch b lying in blocks B - 1, B and B + 1, in order; later entries are arbitrary observations of the batch. `block_count`: the largest is reached in every batch.
All inputs are finite; a program needn't handle non-finite values.
Results may differ from the reference program's by a relative error of at most 0.0001.
Values sent between devices are 32-bit elements; how exact they have to be, the bound alone decides.
A program may use at most 64 MiB of HBM per device.

```python
import math
import jax
import jax.numpy as jnp
from jax import lax

MEMBERS = 256
CELL_BLK = 512
BLK_DEV = 4
OBS_DEV = 64
BLK_OBS = 32
BATCHES = 4
LOC = 96
NBLOCKS = 32
NCELLS = 16384
OBS_B = 512


def layout_batch(key):
    subkeys = jax.random.split(key, 4)
    seat_total = NBLOCKS * BLK_OBS
    seat_ids = jnp.arange(seat_total, dtype=jnp.int32)
    seat_block = seat_ids // BLK_OBS
    dense_dev = jax.random.randint(subkeys[0], (), 0, NBLOCKS // BLK_DEV)
    band_start = jax.random.randint(subkeys[1], (), 0, NBLOCKS)
    in_band = (seat_block - band_start) % NBLOCKS < max(NBLOCKS // 8, 1)
    forced = seat_block // BLK_DEV == dense_dev
    seat_score = jax.random.randint(subkeys[2], (seat_total,), 0, seat_total)
    seat_score = seat_score + seat_total * in_band.astype(jnp.int32) + 2 * seat_total * forced.astype(jnp.int32)
    ranking = jnp.argsort(-seat_score, stable=True)
    chosen = jnp.sort(ranking[:OBS_B])
    home_block = chosen // BLK_OBS
    offset = jax.random.randint(subkeys[3], (OBS_B,), 0, CELL_BLK)
    cell_sorted = (home_block * CELL_BLK + offset).astype(jnp.int32)
    owners = OBS_B // OBS_DEV
    obs_cell = cell_sorted.reshape(OBS_DEV, owners).T.reshape(-1)
    block_ids = jnp.arange(NBLOCKS, dtype=jnp.int32)
    counts = jnp.sum((home_block[None, :] == block_ids[:, None]).astype(jnp.int32), axis=1)
    run_start = jnp.cumsum(counts) - counts
    zero_pad = jnp.zeros((1,), jnp.int32)
    before = jnp.concatenate([zero_pad, counts[:-1]])
    after_count = jnp.concatenate([counts[1:], zero_pad])
    list_start = run_start - before
    position = jnp.clip(list_start[:, None] + jnp.arange(LOC, dtype=jnp.int32)[None, :], 0, OBS_B - 1)
    block_obs = (position % owners * OBS_DEV + position // owners).astype(jnp.int32)
    return (obs_cell, block_obs, (before + counts + after_count).astype(jnp.int32))


def layouts(key):
    batch_keys = jax.random.split(key, BATCHES)
    return jax.vmap(layout_batch)(batch_keys)


def draw_obs_cell(key, part):
    return layouts(key)[0]


def draw_block_obs(key, part):
    return layouts(key)[1]


def draw_block_count(key, part):
    return layouts(key)[2]


def level_of(key, dims, cuts, smallest, high):
    def one(dim, parts):
        steps = jax.random.uniform(jax.random.fold_in(jax.random.fold_in(key, 6), dim), (parts,), jnp.float32, smallest / len(cuts), high / len(cuts))
        return jnp.repeat(jnp.exp(steps), dims[dim] // parts).reshape((-1,) + (1,) * (len(dims) - dim - 1))

    gain = one(*cuts[0])
    for cut in cuts[1:]:
        gain = gain * one(*cut)
    return gain


def bell_draw(key, shape, width, reach, shards=(), kind=jnp.bfloat16):
    gain = level_of(key, shape, shards, -0.22, 0.18) if shards else 1.0
    values = jax.random.normal(key, shape, jnp.float32) * width * gain
    return jnp.minimum(jnp.maximum(values, -reach), reach).astype(kind)


def setup_inputs(seed: int = 0) -> dict:
    key_list = jax.random.split(jax.random.key(seed), 9)
    state_mean = bell_draw(key_list[0], (NCELLS,), 1.0, 6.0, ((0, 8),), jnp.float32)
    state_pert = bell_draw(key_list[1], (MEMBERS, NCELLS), 1.0, 6.0, ((0, 4), (1, 8)), jnp.float32)
    obs_value = bell_draw(key_list[2], (BATCHES, OBS_B), 2.0, 10.0, ((1, 8),), jnp.float32)
    obs_error = jnp.clip(jnp.exp(math.log(2.0) - 2.9957323 * jax.random.uniform(key_list[3], (BATCHES, OBS_B), jnp.float32) ** level_of(key_list[3], (BATCHES, OBS_B), ((1, 8),), -0.2, 0.2)), 0.1, 2.0)
    obs_cell = draw_obs_cell(jax.random.fold_in(key_list[8], 71), 0)
    block_obs = draw_block_obs(jax.random.fold_in(key_list[8], 71), 0)
    block_count = draw_block_count(jax.random.fold_in(key_list[8], 71), 0)
    batch_order = jax.random.permutation(key_list[7], BATCHES).astype(jnp.int32)
    return dict(state_mean=state_mean, state_pert=state_pert, obs_value=obs_value, obs_error=obs_error, obs_cell=obs_cell, block_obs=block_obs, block_count=block_count, batch_order=batch_order)


def taper_weight(distance, radius):
    fraction = distance / radius
    inside = (1.0 - fraction) * (1.0 - fraction) * (1.0 + 2.0 * fraction)
    return jnp.where(fraction < 1.0, inside, jnp.zeros_like(inside))

def reference(state_mean, state_pert, obs_value, obs_error, obs_cell, block_obs, block_count, batch_order):
    mean_state = state_mean
    pert_state = state_pert
    cell_ids = jnp.arange(NCELLS, dtype=jnp.int32).reshape(NBLOCKS, CELL_BLK)
    list_ids = jnp.arange(LOC, dtype=jnp.int32)
    for step_index in range(BATCHES):
        batch_id = batch_order[step_index]
        obs_where = lax.dynamic_index_in_dim(obs_cell, batch_id, 0, keepdims=False)
        values = jnp.take(pert_state, obs_where, axis=1)
        base_mean = jnp.take(mean_state, obs_where)
        col_shift = lax.optimization_barrier(jnp.sum(values, axis=0)) / MEMBERS
        anomaly = values - col_shift[None, :]
        spread = lax.optimization_barrier(jnp.sum(anomaly * anomaly, axis=0)) / (MEMBERS - 1)
        observed = lax.dynamic_index_in_dim(obs_value, batch_id, 0, keepdims=False)
        obs_var = lax.dynamic_index_in_dim(obs_error, batch_id, 0, keepdims=False)
        innovation = observed - (base_mean + col_shift)
        total_var = spread + obs_var
        gain_obs = 1.0 / total_var
        alpha_obs = 1.0 / (1.0 + jnp.sqrt(obs_var / total_var))
        obs_lists = lax.dynamic_index_in_dim(block_obs, batch_id, 0, keepdims=False)
        counts = lax.dynamic_index_in_dim(block_count, batch_id, 0, keepdims=False)
        flat_list = obs_lists.reshape(-1)
        sel_anoms = jnp.take(anomaly, flat_list, axis=1).reshape(MEMBERS, NBLOCKS, LOC)
        innov_list = jnp.take(innovation, flat_list).reshape(NBLOCKS, LOC)
        gain_list = jnp.take(gain_obs, flat_list).reshape(NBLOCKS, LOC)
        alpha_list = jnp.take(alpha_obs, flat_list).reshape(NBLOCKS, LOC)
        where_list = jnp.take(obs_where, flat_list).reshape(NBLOCKS, LOC)
        blocks = pert_state.reshape(MEMBERS, NBLOCKS, CELL_BLK)
        cov_block = jnp.einsum('mbl,mbc->blc', sel_anoms, blocks, precision=lax.Precision.HIGHEST) / (MEMBERS - 1)
        distance = jnp.abs(cell_ids[:, None, :] - where_list[:, :, None]).astype(jnp.float32)
        live_mask = (list_ids[None, :] < counts[:, None]).astype(jnp.float32)
        weight = cov_block * taper_weight(distance, 2.0 * CELL_BLK) * (live_mask * gain_list)[:, :, None]
        mean_state = mean_state + lax.optimization_barrier(jnp.sum(weight * innov_list[:, :, None], axis=1)).reshape(-1)
        update = jnp.einsum('blc,mbl->mbc', weight * alpha_list[:, :, None], sel_anoms, precision=lax.Precision.HIGHEST)
        pert_state = (blocks - update).reshape(MEMBERS, NCELLS)
    return (mean_state, pert_state)
```

```python
import functools

import jax
import jax.numpy as jnp
from jax import lax
from jax.experimental import pallas as pl
from jax.experimental.pallas import tpu as pltpu
from jax.sharding import PartitionSpec as P

MESH = pl.DeviceIdType.MESH
SLOTS = 32
LANES = 128


def split(x):
    hi = x.astype(jnp.bfloat16)
    return hi, (x - hi.astype(jnp.float32)).astype(jnp.bfloat16)


def dot(a, b, dims):
    return lax.dot_general(a, b, (dims, ((), ())), preferred_element_type=jnp.float32)


def dot3(a, b, dims):
    return dot(a[0], b[0], dims) + (dot(a[0], b[1], dims) + dot(a[1], b[0], dims))


def kernel(
    ncells,
    nens,
    order_ref,
    mean_ref,
    pert_ref,
    value_ref,
    error_ref,
    cell_ref,
    mean_out,
    pert_out,
    state,
    state_hi,
    state_lo,
    mean_own,
    obs_mine,
    obs_all,
    cell_own,
    rank_own,
    meta,
    panel,
    in_send,
    in_recv,
    obs_send,
    obs_recv,
    nb_send,
    nb_recv,
    out_send,
    out_recv,
    mout_send,
    mout_recv,
    local_sem,
):
    members, blk = state.shape
    mem_per = members // nens
    batches, obs_per = value_ref.shape
    ci = lax.axis_index("cells")
    ei = lax.axis_index("ens")
    odd = lax.rem(ci, 2)

    def place(e):
        return e + odd * (nens - 1 - 2 * e)

    k = place(ei)
    block = ci * nens + k
    last = ncells * nens - 1
    has_left = block > 0
    has_right = block < last

    barrier = pltpu.get_barrier_semaphore()
    for d in range(1, nens):
        pl.semaphore_signal(
            barrier, inc=1, device_id={"ens": lax.rem(ei + d, nens)}, device_id_type=MESH
        )

    def greet(d, carry):
        pl.semaphore_signal(
            barrier, inc=1, device_id={"cells": lax.rem(ci + d, ncells)}, device_id_type=MESH
        )
        return carry

    lax.fori_loop(1, ncells, greet, 0)

    obs_mine[0:batches, :] = value_ref[...]
    obs_mine[batches : 2 * batches, :] = error_ref[...]
    pl.semaphore_wait(barrier, nens - 1 + ncells - 1)

    def cols(block_k):
        return pl.ds(pl.multiple_of(block_k * blk, blk), blk)

    def rows(e):
        return pl.ds(pl.multiple_of(e * mem_per, mem_per), mem_per)

    in_copies = []
    for d in range(1, nens):
        to = lax.rem(ei + d, nens)
        in_copies.append(
            pltpu.make_async_remote_copy(
                src_ref=pert_ref.at[:, cols(place(to))],
                dst_ref=state.at[rows(ei), :],
                send_sem=in_send.at[d],
                recv_sem=in_recv.at[d],
                device_id={"ens": to},
                device_id_type=MESH,
            )
        )
    for c in in_copies:
        c.start()
    own_in = pltpu.make_async_copy(
        pert_ref.at[:, cols(k)], state.at[rows(ei), :], local_sem.at[0]
    )
    own_in.start()

    def obs_copy(d):
        return pltpu.make_async_remote_copy(
            src_ref=obs_mine,
            dst_ref=obs_all.at[ci],
            send_sem=obs_send.at[d],
            recv_sem=obs_recv.at[d],
            device_id={"cells": lax.rem(ci + d, ncells)},
            device_id_type=MESH,
        )

    def obs_start(d, carry):
        obs_copy(d).start()
        return carry

    lax.fori_loop(1, ncells, obs_start, 0)
    own_obs = pltpu.make_async_copy(obs_mine, obs_all.at[ci], local_sem.at[1])
    own_obs.start()

    lane_a = lax.broadcasted_iota(jnp.int32, (obs_per, obs_per), 0)
    lane_b = lax.broadcasted_iota(jnp.int32, (obs_per, obs_per), 1)
    earlier = (lane_a < lane_b).astype(jnp.bfloat16)
    run = jnp.zeros((batches, 1), jnp.float32)
    for o in range(ncells):
        cells = cell_ref[:, o * obs_per : (o + 1) * obs_per]
        inside = (cells >= block * blk) & (cells < (block + 1) * blk)
        ones = jnp.where(inside, 1.0, 0.0)
        before = dot(ones.astype(jnp.bfloat16), earlier, ((1,), (0,)))
        cell_own[o] = cells
        rank_own[o] = jnp.where(inside, (before + run).astype(jnp.int32), -1)
        run = run + jnp.sum(ones, axis=1, keepdims=True)

    mean_own[...] = mean_ref[:, cols(k)]

    @pl.when(jnp.logical_not(has_left))
    def _():
        for t in range(batches):
            panel[t, 0] = jnp.zeros(panel.shape[2:], jnp.float32)

    @pl.when(jnp.logical_not(has_right))
    def _():
        for t in range(batches):
            panel[t, 2] = jnp.zeros(panel.shape[2:], jnp.float32)

    def obs_wait(d, carry):
        obs_copy(d).wait()
        return carry

    own_obs.wait()
    lax.fori_loop(1, ncells, obs_wait, 0)

    slot_ids = lax.broadcasted_iota(jnp.int32, (SLOTS, obs_per), 0)
    lane_ids = lax.broadcasted_iota(jnp.int32, (SLOTS, LANES), 1)
    for b in range(batches):

        def pick(o, acc):
            hit = rank_own[o, b : b + 1, :] == slot_ids
            cell = cell_own[o, b : b + 1, :]
            value = obs_all[o, b : b + 1, :]
            error = obs_all[o, batches + b : batches + b + 1, :]
            return (
                acc[0] + jnp.where(hit, cell + 1, 0),
                acc[1] + jnp.where(hit, value, 0.0),
                acc[2] + jnp.where(hit, error, 0.0),
            )

        zero = jnp.zeros((SLOTS, obs_per), jnp.float32)
        acc = lax.fori_loop(0, ncells, pick, (zero.astype(jnp.int32), zero, zero), unroll=min(ncells, 8))
        cell = jnp.sum(acc[0].astype(jnp.float32), axis=1, keepdims=True) - 1.0
        value = jnp.sum(acc[1], axis=1, keepdims=True)
        error = jnp.sum(acc[2], axis=1, keepdims=True)
        meta[b] = jnp.where(lane_ids == 0, cell, jnp.where(lane_ids == 1, value, error))

    for c in in_copies:
        c.wait()
    own_in.wait()
    for h in range(0, blk, 256):
        hi, lo = split(state[:, h : h + 256])
        state_hi[:, h : h + 256] = hi
        state_lo[:, h : h + 256] = lo

    left_c = jnp.where(k > 0, ci, ci - 1)
    left_e = jnp.where(k > 0, place(k - 1), ei)
    right_c = jnp.where(k < nens - 1, ci, ci + 1)
    right_e = jnp.where(k < nens - 1, place(k + 1), ei)

    width = 256
    for t in range(batches):
        b = order_ref[t]
        info = meta[b]
        cell = info[:, 0:1]
        value = info[:, 1:2]
        live = cell >= 0.0
        error = jnp.where(live, info[:, 2:3], 1.0)
        ids = lax.broadcasted_iota(jnp.int32, (SLOTS, blk), 1) + block * blk
        here = ids == cell.astype(jnp.int32)
        onehot = jnp.where(here, 1.0, 0.0).astype(jnp.bfloat16)
        values = dot(onehot, state_hi[...], ((1,), (1,))) + dot(
            onehot, state_lo[...], ((1,), (1,))
        )
        base = jnp.sum(jnp.where(here, mean_own[...], 0.0), axis=1, keepdims=True)
        shift = jnp.sum(values, axis=1, keepdims=True) / members
        anomaly = values - shift
        spread = jnp.sum(anomaly * anomaly, axis=1, keepdims=True) / (members - 1)
        innovation = value - (base + shift)
        total = spread + error
        gain = jnp.where(live, 1.0 / total, 0.0)
        alpha = 1.0 / (1.0 + jnp.sqrt(error / total))
        panel[t, 1, :, 0:members] = anomaly
        panel[t, 1, :, members : members + LANES] = jnp.where(
            lane_ids == 0,
            innovation,
            jnp.where(lane_ids == 1, gain, jnp.where(lane_ids == 2, alpha, cell)),
        )
        to_left = pltpu.make_async_remote_copy(
            src_ref=panel.at[t, 1],
            dst_ref=panel.at[t, 2],
            send_sem=nb_send.at[t, 0],
            recv_sem=nb_recv.at[t, 2],
            device_id={"cells": left_c, "ens": left_e},
            device_id_type=MESH,
        )
        to_right = pltpu.make_async_remote_copy(
            src_ref=panel.at[t, 1],
            dst_ref=panel.at[t, 0],
            send_sem=nb_send.at[t, 1],
            recv_sem=nb_recv.at[t, 0],
            device_id={"cells": right_c, "ens": right_e},
            device_id_type=MESH,
        )

        @pl.when(has_left)
        def _():
            to_left.start()

        @pl.when(has_right)
        def _():
            to_right.start()

        @pl.when(has_left)
        def _():
            to_left.wait_send()
            to_right.wait_recv()

        @pl.when(has_right)
        def _():
            to_right.wait_send()
            to_left.wait_recv()

        sel = jnp.concatenate([panel[t, s, :, 0:members] for s in range(3)], axis=0)
        facts = jnp.concatenate(
            [panel[t, s, :, members : members + LANES] for s in range(3)], axis=0
        )
        sel_parts = split(sel)
        sel_t = split(sel.T)
        innov_l = facts[:, 0:1]
        gain_l = facts[:, 1:2] / (members - 1)
        alpha_l = facts[:, 2:3]
        cell_l = facts[:, 3:4]
        for h in range(0, blk, width):
            at = slice(h, h + width)
            cov = dot3(sel_parts, (state_hi[:, at], state_lo[:, at]), ((1,), (0,)))
            ids = lax.broadcasted_iota(jnp.int32, (3 * SLOTS, width), 1) + (block * blk + h)
            f = jnp.abs(ids.astype(jnp.float32) - cell_l) * (1.0 / (2 * blk))
            taper = jnp.where(f < 1.0, (1.0 - f) * (1.0 - f) * (1.0 + 2.0 * f), 0.0)
            weight = cov * taper * gain_l
            mean_own[:, at] = mean_own[:, at] + jnp.sum(weight * innov_l, axis=0, keepdims=True)
            update = dot3(sel_t, split(weight * alpha_l), ((1,), (0,)))
            new = state[:, at] - update
            state[:, at] = new
            if t < batches - 1:
                hi, lo = split(new)
                state_hi[:, at] = hi
                state_lo[:, at] = lo

    out_copies = []
    for d in range(1, nens):
        to = lax.rem(ei + d, nens)
        out_copies.append(
            pltpu.make_async_remote_copy(
                src_ref=state.at[rows(to), :],
                dst_ref=pert_out.at[:, cols(k)],
                send_sem=out_send.at[d],
                recv_sem=out_recv.at[d],
                device_id={"ens": to},
                device_id_type=MESH,
            )
        )
        out_copies.append(
            pltpu.make_async_remote_copy(
                src_ref=mean_own,
                dst_ref=mean_out.at[:, cols(k)],
                send_sem=mout_send.at[d],
                recv_sem=mout_recv.at[d],
                device_id={"ens": to},
                device_id_type=MESH,
            )
        )
    for c in out_copies:
        c.start()
    own_out = [
        pltpu.make_async_copy(state.at[rows(ei), :], pert_out.at[:, cols(k)], local_sem.at[2]),
        pltpu.make_async_copy(mean_own, mean_out.at[:, cols(k)], local_sem.at[3]),
    ]
    for c in own_out:
        c.start()
    for c in own_out + out_copies:
        c.wait()


def shards(ncells, nens, mean, pert, value, error, cell, block_obs, block_count, order):
    mem_per, cell_per = pert.shape
    members = mem_per * nens
    batches, obs_per = value.shape
    blk = cell_per // block_obs.shape[1]
    vmem = pl.BlockSpec(memory_space=pltpu.VMEM)
    smem = pl.BlockSpec(memory_space=pltpu.SMEM)
    anywhere = pl.BlockSpec(memory_space=pl.ANY)
    mean_new, pert_new = pl.pallas_call(
        functools.partial(kernel, ncells, nens),
        out_shape=(
            jax.ShapeDtypeStruct((1, cell_per), jnp.float32),
            jax.ShapeDtypeStruct((mem_per, cell_per), jnp.float32),
        ),
        in_specs=[smem, vmem, anywhere, vmem, vmem, vmem],
        out_specs=(vmem, anywhere),
        scratch_shapes=[
            pltpu.VMEM((members, blk), jnp.float32),
            pltpu.VMEM((members, blk), jnp.bfloat16),
            pltpu.VMEM((members, blk), jnp.bfloat16),
            pltpu.VMEM((1, blk), jnp.float32),
            pltpu.VMEM((2 * batches, obs_per), jnp.float32),
            pltpu.VMEM((ncells, 2 * batches, obs_per), jnp.float32),
            pltpu.VMEM((ncells, batches, obs_per), jnp.int32),
            pltpu.VMEM((ncells, batches, obs_per), jnp.int32),
            pltpu.VMEM((batches, SLOTS, LANES), jnp.float32),
            pltpu.VMEM((batches, 3, SLOTS, members + LANES), jnp.float32),
            pltpu.SemaphoreType.DMA((nens,)),
            pltpu.SemaphoreType.DMA((nens,)),
            pltpu.SemaphoreType.DMA((ncells,)),
            pltpu.SemaphoreType.DMA((ncells,)),
            pltpu.SemaphoreType.DMA((batches, 2)),
            pltpu.SemaphoreType.DMA((batches, 3)),
            pltpu.SemaphoreType.DMA((nens,)),
            pltpu.SemaphoreType.DMA((nens,)),
            pltpu.SemaphoreType.DMA((nens,)),
            pltpu.SemaphoreType.DMA((nens,)),
            pltpu.SemaphoreType.DMA((4,)),
        ],
        compiler_params=pltpu.CompilerParams(
            collective_id=0, has_side_effects=True, vmem_limit_bytes=32 * 1024 * 1024
        ),
    )(order, mean.reshape(1, cell_per), pert, value, error, cell)
    return mean_new.reshape(cell_per), pert_new


def solution(mesh):
    placed = (
        P("cells"),
        P("ens", "cells"),
        P(None, "cells"),
        P(None, "cells"),
        P(),
        P(None, "cells", None),
        P(None, "cells"),
        P(),
    )
    return jax.shard_map(
        functools.partial(shards, mesh.shape["cells"], mesh.shape["ens"]),
        mesh=mesh,
        in_specs=placed,
        out_specs=(P("cells"), P("ens", "cells")),
        check_vma=False,
    )
```

```python
import functools

import jax
import jax.numpy as jnp
from jax import lax
from jax.experimental import pallas as pl
from jax.experimental.pallas import tpu as pltpu
from jax.sharding import PartitionSpec as P

MESH = pl.DeviceIdType.MESH
SLOTS = 32
LANES = 128


def split(x):
    hi = x.astype(jnp.bfloat16)
    return hi, (x - hi.astype(jnp.float32)).astype(jnp.bfloat16)


def dot(a, b, dims):
    return lax.dot_general(a, b, (dims, ((), ())), preferred_element_type=jnp.float32)


def dot3(a, b, dims):
    return dot(a[0], b[0], dims) + (dot(a[0], b[1], dims) + dot(a[1], b[0], dims))


def kernel(
    ncells,
    nens,
    order_ref,
    mean_ref,
    pert_ref,
    value_ref,
    error_ref,
    cell_hbm,
    mean_out,
    pert_out,
    state,
    state_hi,
    state_lo,
    mean_own,
    cell_ref,
    obs_mine,
    obs_all,
    cell_own,
    rank_own,
    meta,
    panel,
    in_send,
    in_recv,
    obs_send,
    obs_recv,
    nb_send,
    nb_recv,
    out_send,
    out_recv,
    mout_send,
    mout_recv,
    local_sem,
):
    members, blk = state.shape
    mem_per = members // nens
    batches, obs_per = value_ref.shape
    ci = lax.axis_index("cells")
    ei = lax.axis_index("ens")
    odd = lax.rem(ci, 2)

    def place(e):
        return e + odd * (nens - 1 - 2 * e)

    k = place(ei)
    block = ci * nens + k
    last = ncells * nens - 1
    has_left = block > 0
    has_right = block < last

    def cols(block_k):
        return pl.ds(pl.multiple_of(block_k * blk, blk), blk)

    loads = [
        pltpu.make_async_copy(value_ref, obs_mine.at[0:batches, :], local_sem.at[4]),
        pltpu.make_async_copy(error_ref, obs_mine.at[batches : 2 * batches, :], local_sem.at[5]),
        pltpu.make_async_copy(cell_hbm, cell_ref, local_sem.at[6]),
        pltpu.make_async_copy(mean_ref.at[:, cols(k)], mean_own, local_sem.at[7]),
    ]
    for c in loads:
        c.start()
    barrier = pltpu.get_barrier_semaphore()
    for d in range(1, nens):
        pl.semaphore_signal(
            barrier, inc=1, device_id={"ens": lax.rem(ei + d, nens)}, device_id_type=MESH
        )

    def greet(d, carry):
        pl.semaphore_signal(
            barrier, inc=1, device_id={"cells": lax.rem(ci + d, ncells)}, device_id_type=MESH
        )
        return carry

    lax.fori_loop(1, ncells, greet, 0)

    pl.semaphore_wait(barrier, nens - 1 + ncells - 1)

    def rows(e):
        return pl.ds(pl.multiple_of(e * mem_per, mem_per), mem_per)

    in_copies = []
    for d in range(1, nens):
        to = lax.rem(ei + d, nens)
        in_copies.append(
            pltpu.make_async_remote_copy(
                src_ref=pert_ref.at[:, cols(place(to))],
                dst_ref=state.at[rows(ei), :],
                send_sem=in_send.at[d],
                recv_sem=in_recv.at[d],
                device_id={"ens": to},
                device_id_type=MESH,
            )
        )
    for c in in_copies:
        c.start()
    own_in = pltpu.make_async_copy(
        pert_ref.at[:, cols(k)], state.at[rows(ei), :], local_sem.at[0]
    )
    own_in.start()
    for c in loads:
        c.wait()

    def obs_copy(d):
        return pltpu.make_async_remote_copy(
            src_ref=obs_mine,
            dst_ref=obs_all.at[ci],
            send_sem=obs_send.at[d],
            recv_sem=obs_recv.at[d],
            device_id={"cells": lax.rem(ci + d, ncells)},
            device_id_type=MESH,
        )

    def obs_start(d, carry):
        obs_copy(d).start()
        return carry

    lax.fori_loop(1, ncells, obs_start, 0)
    own_obs = pltpu.make_async_copy(obs_mine, obs_all.at[ci], local_sem.at[1])
    own_obs.start()

    lane_a = lax.broadcasted_iota(jnp.int32, (obs_per, obs_per), 0)
    lane_b = lax.broadcasted_iota(jnp.int32, (obs_per, obs_per), 1)
    earlier = (lane_a < lane_b).astype(jnp.bfloat16)
    run = jnp.zeros((batches, 1), jnp.float32)
    for o in range(ncells):
        cells = cell_ref[:, o * obs_per : (o + 1) * obs_per]
        inside = (cells >= block * blk) & (cells < (block + 1) * blk)
        ones = jnp.where(inside, 1.0, 0.0)
        before = dot(ones.astype(jnp.bfloat16), earlier, ((1,), (0,)))
        cell_own[o] = cells
        rank_own[o] = jnp.where(inside, (before + run).astype(jnp.int32), -1)
        run = run + jnp.sum(ones, axis=1, keepdims=True)

    @pl.when(jnp.logical_not(has_left))
    def _():
        for t in range(batches):
            panel[t, 0] = jnp.zeros(panel.shape[2:], jnp.float32)

    @pl.when(jnp.logical_not(has_right))
    def _():
        for t in range(batches):
            panel[t, 2] = jnp.zeros(panel.shape[2:], jnp.float32)

    def obs_wait(d, carry):
        obs_copy(d).wait()
        return carry

    own_obs.wait()
    lax.fori_loop(1, ncells, obs_wait, 0)

    slot_ids = lax.broadcasted_iota(jnp.int32, (SLOTS, obs_per), 0)
    lane_ids = lax.broadcasted_iota(jnp.int32, (SLOTS, LANES), 1)
    for b in range(batches):

        def pick(o, acc):
            hit = rank_own[o, b : b + 1, :] == slot_ids
            cell = cell_own[o, b : b + 1, :]
            value = obs_all[o, b : b + 1, :]
            error = obs_all[o, batches + b : batches + b + 1, :]
            return (
                acc[0] + jnp.where(hit, cell + 1, 0),
                acc[1] + jnp.where(hit, value, 0.0),
                acc[2] + jnp.where(hit, error, 0.0),
            )

        zero = jnp.zeros((SLOTS, obs_per), jnp.float32)
        acc = lax.fori_loop(0, ncells, pick, (zero.astype(jnp.int32), zero, zero), unroll=min(ncells, 8))
        cell = jnp.sum(acc[0].astype(jnp.float32), axis=1, keepdims=True) - 1.0
        value = jnp.sum(acc[1], axis=1, keepdims=True)
        error = jnp.sum(acc[2], axis=1, keepdims=True)
        meta[b] = jnp.where(lane_ids == 0, cell, jnp.where(lane_ids == 1, value, error))

    for c in in_copies:
        c.wait()
    own_in.wait()
    for h in range(0, blk, 256):
        hi, lo = split(state[:, h : h + 256])
        state_hi[:, h : h + 256] = hi
        state_lo[:, h : h + 256] = lo

    left_c = jnp.where(k > 0, ci, ci - 1)
    left_e = jnp.where(k > 0, place(k - 1), ei)
    right_c = jnp.where(k < nens - 1, ci, ci + 1)
    right_e = jnp.where(k < nens - 1, place(k + 1), ei)

    width = 256
    out_copies, own_out = [], []
    for t in range(batches):
        b = order_ref[t]
        info = meta[b]
        cell = info[:, 0:1]
        value = info[:, 1:2]
        live = cell >= 0.0
        error = jnp.where(live, info[:, 2:3], 1.0)
        ids = lax.broadcasted_iota(jnp.int32, (SLOTS, blk), 1) + block * blk
        here = ids == cell.astype(jnp.int32)
        onehot = jnp.where(here, 1.0, 0.0).astype(jnp.bfloat16)
        values = dot(onehot, state_hi[...], ((1,), (1,))) + dot(
            onehot, state_lo[...], ((1,), (1,))
        )
        base = jnp.sum(jnp.where(here, mean_own[...], 0.0), axis=1, keepdims=True)
        shift = jnp.sum(values, axis=1, keepdims=True) / members
        anomaly = values - shift
        spread = jnp.sum(anomaly * anomaly, axis=1, keepdims=True) / (members - 1)
        innovation = value - (base + shift)
        total = spread + error
        gain = jnp.where(live, 1.0 / total, 0.0)
        alpha = 1.0 / (1.0 + jnp.sqrt(error / total))
        panel[t, 1, :, 0:members] = anomaly
        panel[t, 1, :, members : members + LANES] = jnp.where(
            lane_ids == 0,
            innovation,
            jnp.where(lane_ids == 1, gain, jnp.where(lane_ids == 2, alpha, cell)),
        )
        to_left = pltpu.make_async_remote_copy(
            src_ref=panel.at[t, 1],
            dst_ref=panel.at[t, 2],
            send_sem=nb_send.at[t, 0],
            recv_sem=nb_recv.at[t, 2],
            device_id={"cells": left_c, "ens": left_e},
            device_id_type=MESH,
        )
        to_right = pltpu.make_async_remote_copy(
            src_ref=panel.at[t, 1],
            dst_ref=panel.at[t, 0],
            send_sem=nb_send.at[t, 1],
            recv_sem=nb_recv.at[t, 0],
            device_id={"cells": right_c, "ens": right_e},
            device_id_type=MESH,
        )

        @pl.when(has_left)
        def _():
            to_left.start()

        @pl.when(has_right)
        def _():
            to_right.start()

        @pl.when(has_left)
        def _():
            to_left.wait_send()
            to_right.wait_recv()

        @pl.when(has_right)
        def _():
            to_right.wait_send()
            to_left.wait_recv()

        sel = jnp.concatenate([panel[t, s, :, 0:members] for s in range(3)], axis=0)
        facts = jnp.concatenate(
            [panel[t, s, :, members : members + LANES] for s in range(3)], axis=0
        )
        sel_parts = split(sel)
        sel_t = split(sel.T)
        innov_l = facts[:, 0:1]
        gain_l = facts[:, 1:2] / (members - 1)
        alpha_l = facts[:, 2:3]
        cell_l = facts[:, 3:4]
        for h in range(0, blk, width):
            at = slice(h, h + width)
            cov = dot3(sel_parts, (state_hi[:, at], state_lo[:, at]), ((1,), (0,)))
            ids = lax.broadcasted_iota(jnp.int32, (3 * SLOTS, width), 1) + (block * blk + h)
            f = jnp.abs(ids.astype(jnp.float32) - cell_l) * (1.0 / (2 * blk))
            taper = jnp.where(f < 1.0, (1.0 - f) * (1.0 - f) * (1.0 + 2.0 * f), 0.0)
            weight = cov * taper * gain_l
            mean_own[:, at] = mean_own[:, at] + jnp.sum(weight * innov_l, axis=0, keepdims=True)
            update = dot3(sel_t, split(weight * alpha_l), ((1,), (0,)))
            new = state[:, at] - update
            state[:, at] = new
            if t < batches - 1:
                hi, lo = split(new)
                state_hi[:, at] = hi
                state_lo[:, at] = lo
                continue
            part = h // width
            there = pl.ds(pl.multiple_of(k * blk + h, width), width)
            for d in range(1, nens):
                to = lax.rem(ei + d, nens)
                out_copies.append(
                    pltpu.make_async_remote_copy(
                        src_ref=state.at[rows(to), pl.ds(h, width)],
                        dst_ref=pert_out.at[:, there],
                        send_sem=out_send.at[part, d],
                        recv_sem=out_recv.at[part, d],
                        device_id={"ens": to},
                        device_id_type=MESH,
                    )
                )
                out_copies[-1].start()
            own_out.append(
                pltpu.make_async_copy(
                    state.at[rows(ei), pl.ds(h, width)], pert_out.at[:, there], local_sem.at[8 + part]
                )
            )
            own_out[-1].start()

    for d in range(1, nens):
        out_copies.append(
            pltpu.make_async_remote_copy(
                src_ref=mean_own,
                dst_ref=mean_out.at[:, cols(k)],
                send_sem=mout_send.at[d],
                recv_sem=mout_recv.at[d],
                device_id={"ens": lax.rem(ei + d, nens)},
                device_id_type=MESH,
            )
        )
        out_copies[-1].start()
    own_out.append(pltpu.make_async_copy(mean_own, mean_out.at[:, cols(k)], local_sem.at[3]))
    own_out[-1].start()
    for c in own_out + out_copies:
        c.wait()


def shards(ncells, nens, mean, pert, value, error, cell, block_obs, block_count, order):
    mem_per, cell_per = pert.shape
    members = mem_per * nens
    batches, obs_per = value.shape
    blk = cell_per // block_obs.shape[1]
    vmem = pl.BlockSpec(memory_space=pltpu.VMEM)
    smem = pl.BlockSpec(memory_space=pltpu.SMEM)
    hbm = pl.BlockSpec(memory_space=pltpu.HBM)
    anywhere = pl.BlockSpec(memory_space=pl.ANY)
    mean_new, pert_new = pl.pallas_call(
        functools.partial(kernel, ncells, nens),
        out_shape=(
            jax.ShapeDtypeStruct((1, cell_per), jnp.float32),
            jax.ShapeDtypeStruct((mem_per, cell_per), jnp.float32),
        ),
        in_specs=[smem] + [hbm] * 5,
        out_specs=(vmem, anywhere),
        scratch_shapes=[
            pltpu.VMEM((members, blk), jnp.float32),
            pltpu.VMEM((members, blk), jnp.bfloat16),
            pltpu.VMEM((members, blk), jnp.bfloat16),
            pltpu.VMEM((1, blk), jnp.float32),
            pltpu.VMEM(cell.shape, jnp.int32),
            pltpu.VMEM((2 * batches, obs_per), jnp.float32),
            pltpu.VMEM((ncells, 2 * batches, obs_per), jnp.float32),
            pltpu.VMEM((ncells, batches, obs_per), jnp.int32),
            pltpu.VMEM((ncells, batches, obs_per), jnp.int32),
            pltpu.VMEM((batches, SLOTS, LANES), jnp.float32),
            pltpu.VMEM((batches, 3, SLOTS, members + LANES), jnp.float32),
            pltpu.SemaphoreType.DMA((nens,)),
            pltpu.SemaphoreType.DMA((nens,)),
            pltpu.SemaphoreType.DMA((ncells,)),
            pltpu.SemaphoreType.DMA((ncells,)),
            pltpu.SemaphoreType.DMA((batches, 2)),
            pltpu.SemaphoreType.DMA((batches, 3)),
            pltpu.SemaphoreType.DMA((blk // 256, nens)),
            pltpu.SemaphoreType.DMA((blk // 256, nens)),
            pltpu.SemaphoreType.DMA((nens,)),
            pltpu.SemaphoreType.DMA((nens,)),
            pltpu.SemaphoreType.DMA((8 + blk // 256,)),
        ],
        compiler_params=pltpu.CompilerParams(
            collective_id=0, has_side_effects=True, vmem_limit_bytes=32 * 1024 * 1024
        ),
    )(order, mean.reshape(1, cell_per), pert, value, error, cell)
    return mean_new.reshape(cell_per), pert_new


def solution(mesh):
    placed = (
        P("cells"),
        P("ens", "cells"),
        P(None, "cells"),
        P(None, "cells"),
        P(),
        P(None, "cells", None),
        P(None, "cells"),
        P(),
    )
    return jax.shard_map(
        functools.partial(shards, mesh.shape["cells"], mesh.shape["ens"]),
        mesh=mesh,
        in_specs=placed,
        out_specs=(P("cells"), P("ens", "cells")),
        check_vma=False,
    )
```
